256 devices in a mesh: ctx: 64 (over y, x, z_hi, core), tp: 4 (over z_lo).
Axes of the slice: x: 4, y: 4, z: 8 (z_hi: 2, z_lo: 4; z = z_hi * 4 + z_lo), core: 2. Of those that a mesh axis runs over, the one named last changes fastest.
Arguments:
- query_proj: bfloat16 [16384, 1024], P('ctx', 'tp'), may hold values from -4 to 4
- key_proj: bfloat16 [16384, 1024], P('ctx', 'tp'), may hold values from -4 to 4
- value_proj: bfloat16 [16384, 1024], P('ctx', 'tp'), may hold values from -4 to 4
- filter_taps: float32 [16384, 1024], P('ctx', 'tp'), may hold values from -1.5 to 1.5
- skip_bias: float32 [1024], P('tp'), may hold values from -2.5 to 2.5
- cotangent: bfloat16 [16384, 1024], P('ctx', 'tp'), may hold values from -4 to 4
Outputs:
- gated: bfloat16 [16384, 1024], P('ctx', 'tp')
- grad_query: bfloat16 [16384, 1024], P('ctx', 'tp')
- grad_key: bfloat16 [16384, 1024], P('ctx', 'tp')
- grad_value: bfloat16 [16384, 1024], P('ctx', 'tp')
- grad_taps: float32 [16384, 1024], P('ctx', 'tp')
- grad_skip: float32 [1024], P('tp')
The draws below stay inside these ranges and needn't reach their ends.
All inputs are finite; a program needn't handle non-finite values.
Results may differ from the reference program's by a relative error of at most 0.001.
Values sent between devices are 32-bit elements; how exact they have to be, the bound alone decides.
A program may use at most 128 MiB of HBM per device.

```python
import math
import jax
import jax.numpy as jnp
from jax import lax

TOKENS = 16384
CONV_FEATURES = 1024


def draw_filter_taps(key, part):
    key = jax.random.fold_in(key, 7)
    key_reach, key_noise, key_spots, key_keep = jax.random.split(key, 4)
    kernel_extent = TOKENS
    fading_lags = jnp.arange(kernel_extent, dtype=jnp.float32)[:, None]
    fading_span = jnp.exp(jax.random.uniform(key_reach, (CONV_FEATURES,), jnp.float32, math.log(30.0), math.log(32.0 * kernel_extent)))
    noise = jnp.clip(jax.random.normal(key_noise, (kernel_extent, CONV_FEATURES), jnp.float32), -5.0, 5.0)
    kernel_locations = jax.random.uniform(key_spots, (3, CONV_FEATURES), jnp.float32) * kernel_extent
    retained_selector = jax.random.uniform(key_keep, (3, CONV_FEATURES), jnp.float32, 0.5, 0.8)
    spike_response = jnp.ones((kernel_extent, CONV_FEATURES), jnp.float32)
    for lag_ordinal in range(3):
        spike_response = spike_response * jnp.where(fading_lags >= kernel_locations[lag_ordinal][None, :], retained_selector[lag_ordinal][None, :], 1.0)
    fading_magnitude = jnp.exp(-fading_lags / fading_span[None, :]) * spike_response * jax.lax.rsqrt(0.5 * jnp.minimum(fading_span, float(kernel_extent)) + 1.0)[None, :]
    return (noise * fading_magnitude).astype(jnp.float32)


def shard_levels(key, shape, cuts, smallest, largest):
    def one(position, parts):
        heights = jax.random.uniform(jax.random.fold_in(jax.random.fold_in(key, 6), position), (parts,), jnp.float32, smallest / len(cuts), largest / len(cuts))
        return jnp.repeat(jnp.exp(heights), shape[position] // parts).reshape((-1,) + (1,) * (len(shape) - position - 1))

    level = one(*cuts[0])
    for cut in cuts[1:]:
        level = level * one(*cut)
    return level


def scatter_about(stream_key, extent, deviation, limit, cuts=(), held_as=jnp.bfloat16):
    gain = shard_levels(stream_key, extent, cuts, -0.22, 0.18) if cuts else 1.0
    result = jax.random.normal(stream_key, extent, jnp.float32) * deviation * gain
    return jnp.minimum(jnp.maximum(result, -limit), limit).astype(held_as)


def setup_inputs(seed: int = 0) -> dict:
    key_list = jax.random.split(jax.random.key(seed), 7)
    return {
        "query_proj": scatter_about(key_list[0], (TOKENS, CONV_FEATURES), 1.0, 4.0, ((0, 64), (1, 4))),
        "key_proj": scatter_about(key_list[1], (TOKENS, CONV_FEATURES), 1.0, 4.0, ((0, 64), (1, 4))),
        "value_proj": scatter_about(key_list[2], (TOKENS, CONV_FEATURES), 1.0, 4.0, ((0, 64), (1, 4))),
        "filter_taps": draw_filter_taps(jax.random.fold_in(key_list[6], 71), 0),
        "skip_bias": scatter_about(key_list[4], (CONV_FEATURES,), 0.5, 2.5, ((0, 4),), jnp.float32),
        "cotangent": scatter_about(key_list[5], (TOKENS, CONV_FEATURES), 1.0, 4.0, ((0, 64), (1, 4))),
    }


def spectrum(field):
    return jnp.fft.rfft(field, n=2 * TOKENS, axis=0)

def to_time(spec_field):
    return jnp.fft.irfft(spec_field, n=2 * TOKENS, axis=0)[:TOKENS]

def block_terms(pieces):
    query_proj, key_proj, value_proj, filter_taps, skip_bias, cotangent = pieces
    query32 = query_proj.astype(jnp.float32)
    key32 = key_proj.astype(jnp.float32)
    value32 = value_proj.astype(jnp.float32)
    cot32 = cotangent.astype(jnp.float32)
    inputs = key32 * value32
    spec_inputs = spectrum(inputs)
    spec_taps = spectrum(filter_taps)
    mixed = to_time(spec_inputs * spec_taps) + skip_bias * inputs
    gated = (query32 * mixed).astype(jnp.bfloat16)
    grad_query = (cot32 * mixed).astype(jnp.bfloat16)
    grad_conv = cot32 * query32
    spec_grad = spectrum(grad_conv)
    grad_inputs = to_time(jnp.conj(spec_taps) * spec_grad) + skip_bias * grad_conv
    grad_key = (grad_inputs * value32).astype(jnp.bfloat16)
    grad_value = (grad_inputs * key32).astype(jnp.bfloat16)
    grad_scale = 1.0 / math.sqrt(TOKENS)
    grad_taps = to_time(jnp.conj(spec_inputs) * spec_grad) * grad_scale
    grad_skip = lax.optimization_barrier(jnp.sum(grad_conv * inputs, axis=0)) * grad_scale
    return (gated, grad_query, grad_key, grad_value, grad_taps, grad_skip)

def reference(query_proj, key_proj, value_proj, filter_taps, skip_bias, cotangent):
    width = math.gcd(CONV_FEATURES, 128)
    count = CONV_FEATURES // width

    def split(array):
        return jnp.transpose(array.reshape(TOKENS, count, width), (1, 0, 2))

    def join(array):
        return jnp.transpose(array, (1, 0, 2)).reshape(TOKENS, CONV_FEATURES)
    results = lax.map(block_terms, (split(query_proj), split(key_proj), split(value_proj), split(filter_taps), skip_bias.reshape(count, width), split(cotangent)))
    gated, grad_query, grad_key, grad_value, grad_taps, grad_skip = results
    return (join(gated), join(grad_query), join(grad_key), join(grad_value), join(grad_taps), grad_skip.reshape(CONV_FEATURES))
```

```python
import math

import jax
import jax.numpy as jnp
import numpy as np
from jax import lax
from jax.sharding import PartitionSpec as P

HI = lax.Precision.HIGH
HALF = 128


def tables():
    n = np.arange(HALF)
    k = np.arange(HALF) + 0.5
    period = 2 * HALF * HALF
    a1 = 2 * np.pi * np.outer(k, n) / (2 * HALF)
    at = 2 * np.pi * np.outer(k, n) / period
    a2 = 2 * np.pi * np.outer(n, np.arange(HALF)) / HALF
    c2, s2 = np.cos(a2), np.sin(a2)
    f1 = np.concatenate([np.cos(a1), -np.sin(a1)], 0)
    f2 = np.block([[c2, -s2], [s2, c2]])
    g2 = np.block([[c2, s2], [-s2, c2]])
    g1 = np.concatenate([np.cos(a1).T, -np.sin(a1).T], 1) * (2 / period)
    return [np.asarray(t, np.float32) for t in (f1, f2, g1, g2, np.cos(at), -np.sin(at))]


def shards(query_proj, key_proj, value_proj, filter_taps, skip_bias, cotangent):
    f1, f2, g1, g2, tr, ti = [jnp.asarray(t) for t in tables()]
    q = query_proj.astype(jnp.float32)
    k = key_proj.astype(jnp.float32)
    v = value_proj.astype(jnp.float32)
    ct = cotangent.astype(jnp.float32)
    u = k * v
    gc = ct * q
    n = lax.axis_size("ctx")
    rows, width = u.shape
    each = width // n

    def out(x):
        x = x.T.reshape(n, each, rows)
        x = lax.all_to_all(x, "ctx", split_axis=0, concat_axis=0, tiled=True)
        return jnp.transpose(x.reshape(n, each, rows // HALF, HALF), (1, 0, 2, 3)).reshape(each, HALF, HALF)

    def back(x):
        x = jnp.transpose(x.reshape(each, n, rows // HALF, HALF), (1, 0, 2, 3)).reshape(n, each, rows)
        x = lax.all_to_all(x, "ctx", split_axis=0, concat_axis=0, tiled=True)
        return x.reshape(width, rows).T

    def fwd(x):
        a = jnp.einsum("kn,cnm->ckm", f1, x, precision=HI)
        ar, ai = a[:, :HALF], a[:, HALF:]
        b = jnp.concatenate([ar * tr - ai * ti, ar * ti + ai * tr], 2)
        b = jnp.einsum("ckm,mj->ckj", b, f2, precision=HI)
        return b[..., :HALF], b[..., HALF:]

    def inv(r, i):
        d = jnp.einsum("ckm,mj->ckj", jnp.concatenate([r, i], 2), g2, precision=HI)
        dr, di = d[..., :HALF], d[..., HALF:]
        e = jnp.concatenate([dr * tr + di * ti, di * tr - dr * ti], 1)
        return jnp.einsum("nk,ckm->cnm", g1, e, precision=HI)

    ur, ui = fwd(out(u))
    hr, hi = fwd(out(filter_taps))
    gr, gi = fwd(out(gc))
    conv = back(inv(ur * hr - ui * hi, ur * hi + ui * hr))
    conv_back = back(inv(hr * gr + hi * gi, hr * gi - hi * gr))
    taps_back = back(inv(ur * gr + ui * gi, ur * gi - ui * gr))
    mixed = conv + skip_bias * u
    grad_inputs = conv_back + skip_bias * gc
    scale = 1.0 / math.sqrt(rows * n)
    grad_skip = lax.psum(jnp.sum(gc * u, axis=0), "ctx") * scale
    bf = jnp.bfloat16
    return (
        (q * mixed).astype(bf),
        (ct * mixed).astype(bf),
        (grad_inputs * v).astype(bf),
        (grad_inputs * k).astype(bf),
        taps_back * scale,
        grad_skip,
    )


def solution(mesh):
    s = P("ctx", "tp")
    return jax.shard_map(
        shards, mesh=mesh, in_specs=(s, s, s, s, P("tp"), s), out_specs=(s, s, s, s, s, P("tp")), check_vma=False
    )
```

```python
import math

import jax
import jax.numpy as jnp
import numpy as np
from jax import lax
from jax.experimental import pallas as pl
from jax.experimental.pallas import tpu as pltpu
from jax.sharding import PartitionSpec as P

MESH = pl.DeviceIdType.MESH
F32 = jnp.float32
BF16 = jnp.bfloat16
HALF = 128
PLANE = 32
TILE = 8
BLOCK = PLANE * TILE
ROWS = 2 * BLOCK


def tables():
    half, z, source = np.meshgrid(np.arange(2), np.arange(2), np.arange(PLANE), indexing="ij")
    block = (source // 2) * 4 + z * 2 + source % 2
    n1 = (block * 2 + half).reshape(-1)
    k1 = np.arange(HALF) + 0.5
    n2 = np.arange(HALF)
    period = 2 * HALF * HALF
    first = 2 * np.pi * np.outer(k1, n1) / (2 * HALF)
    twist = 2 * np.pi * np.outer(k1, n2) / period
    second = 2 * np.pi * np.outer(n2, np.arange(HALF)) / HALF
    c2, s2 = np.cos(second), np.sin(second)
    f1 = np.concatenate([np.cos(first), -np.sin(first)], 0)
    f2 = np.block([[c2, -s2], [s2, c2]])
    g2 = np.block([[c2, s2], [-s2, c2]])
    g1 = np.concatenate([np.cos(first).T, -np.sin(first).T], 1) * (2 / period)
    return [t.astype(np.float32) for t in (f1, f2, g1, g2, np.cos(twist), -np.sin(twist))]


def split(x):
    high = x.astype(BF16)
    return high, (x - high.astype(F32)).astype(BF16)


def dot(a, b):
    return jnp.dot(a, b, preferred_element_type=F32)


def dot3(a, b):
    return dot(a[0], b[0]) + (dot(a[0], b[1]) + dot(a[1], b[0]))


def kernel(
    q_in, k_in, v_in, taps_in, skip_in, cot_in,
    f1_in, f2_in, g1_in, g2_in, tr_in, ti_in,
    gated_out, gq_out, gk_out, gv_out, gt_out, gs_out,
    q, k, v, taps, skip, cot,
    f1, f2, g1, g2, tr, ti,
    gated, gq, gk, gv, gt, gs,
    sa1, sa2, sa3, sb1, sb2, sb3,
    ea1, ea2, ea3, eb1, eb2, eb3,
    ra1, ra2, ra3, rb1, rb2, rb3,
    spec_u, spec_h, spec_g,
    skip_send, skip_recv, f1h, f1l, f2h, f2l, g1h, g1l, g2h, g2l,
    load_sem, store_sem, z_send, z_recv, own_send, fwd_send, plane_recv, mid_recv, sk_send, sk_recv,
):
    ctx = lax.axis_index("ctx")
    core, mz, yx = ctx % 2, (ctx // 2) % 2, ctx // 4
    oz = 1 - mz
    me = yx * 2 + core
    yblk, m8 = me // 8, me % 8
    x, y = yx % 4, yx // 4

    def plane_device(p):
        return {"ctx": (p // 2) * 4 + mz * 2 + p % 2}

    def peer(t):
        return ((yblk + t // 8) % 4) * 8 + (m8 + t % 8) % 8

    z_device = {"ctx": yx * 4 + oz * 2 + core}

    def rows(start, count):
        return pl.ds(pl.multiple_of(start, TILE), count)

    barrier = pltpu.get_barrier_semaphore()

    def greet(t, carry):
        pl.semaphore_signal(barrier, inc=1, device_id=plane_device(peer(t)), device_id_type=MESH)
        return carry

    sources = (k_in, v_in, taps_in, q_in, cot_in, f1_in, f2_in, g2_in, g1_in, tr_in, ti_in, skip_in)
    targets = (k, v, taps, q, cot, f1, f2, g2, g1, tr, ti, skip)
    loads = [pltpu.make_async_copy(s, t, load_sem.at[i]) for i, (s, t) in enumerate(zip(sources, targets))]
    for load in loads:
        load.start()
    pl.semaphore_signal(barrier, inc=1, device_id=z_device, device_id_type=MESH)
    lax.fori_loop(1, PLANE, greet, 0)

    def wait_rows(ref, count, sem):
        pltpu.make_async_copy(ref.at[pl.ds(0, count)], ref.at[pl.ds(0, count)], sem).wait()

    def plane_sends(src, src_base, dst, dst_row, send_sem, recv_sem, lo=1, hi=PLANE):
        def body(t, carry):
            p = peer(t)
            pltpu.make_async_remote_copy(
                src_ref=src.at[rows(src_base + p * TILE, TILE)],
                dst_ref=dst.at[rows(dst_row, TILE)],
                send_sem=send_sem,
                recv_sem=recv_sem,
                device_id=plane_device(p),
                device_id_type=MESH,
            ).start()
            return carry

        if lo == 1:
            dst[rows(dst_row, TILE), :] = src[rows(src_base + me * TILE, TILE), :]
        lax.fori_loop(lo, hi, body, 0)

    CHUNKS = 4
    CROWS = BLOCK // CHUNKS

    def z_copy(s, e, i, j):
        start = ((yblk + j) % CHUNKS) * CROWS
        return pltpu.make_async_remote_copy(
            src_ref=s.at[rows(oz * BLOCK + start, CROWS)],
            dst_ref=e.at[rows(start, CROWS)],
            send_sem=z_send.at[i, j],
            recv_sem=z_recv.at[i, j],
            device_id=z_device,
            device_id_type=MESH,
        )

    def z_first(i, s, e, r):
        for j in range(CHUNKS):
            z_copy(s, e, i, j).start()
        plane_sends(s, mz * BLOCK, r, (mz * PLANE + me) * TILE, own_send.at[i], plane_recv.at[i])

    def forward(i, s, e, r):
        for j in range(CHUNKS):
            z_copy(s, e, i, j).wait_recv()
            plane_sends(e, 0, r, (oz * PLANE + me) * TILE, fwd_send.at[i], plane_recv.at[i],
                        max(1, 8 * j), 8 * (j + 1))

    def arrived(i, r):
        wait_rows(r, 2 * (BLOCK - TILE), plane_recv.at[i])

    def drain(i, s, e, r):
        for j in range(CHUNKS):
            z_copy(s, e, i, j).wait_send()
        wait_rows(r, BLOCK - TILE, own_send.at[i])
        wait_rows(r, BLOCK - TILE, fwd_send.at[i])

    def put(s, fs, values, h):
        flipped = values.T
        for c in range(2):
            s[pl.ds(fs * 4 + c * 2 + h, 64, stride=TILE), :] = flipped[c * 64 : (c + 1) * 64]

    def piece(ref, h, pair):
        return ref[h * HALF : (h + 1) * HALF, pair * HALF : (pair + 1) * HALF].astype(F32)

    def put_inputs(s, pair):
        for h in range(2):
            put(s, 0, piece(k, h, pair) * piece(v, h, pair), h)
            put(s, 1, piece(taps, h, pair), h)

    def put_grad(s):
        for pair in range(2):
            for h in range(2):
                put(s, pair, piece(q, h, pair) * piece(cot, h, pair), h)

    def forward_pair(r, fs, spec, pair):
        series = []
        for c in range(2):
            parts = [r[pl.ds(z * BLOCK + fs * 4 + c * 2 + h, PLANE, stride=TILE), :] for h in range(2) for z in range(2)]
            series.append(jnp.concatenate(parts, 0))
        a = dot3((f1h[...], f1l[...]), split(jnp.concatenate(series, 1)))
        tc, ts = tr[...], ti[...]
        turned = []
        for c in range(2):
            ar, ai = a[:HALF, c * HALF : (c + 1) * HALF], a[HALF:, c * HALF : (c + 1) * HALF]
            turned.append(jnp.concatenate([ar * tc - ai * ts, ar * ts + ai * tc], 1))
        b = dot3(split(jnp.concatenate(turned, 0)), (f2h[...], f2l[...]))
        for c in range(2):
            spec[pair * 2 + c] = b[c * HALF : (c + 1) * HALF]

    def inverse_pair(a, b, pair, conj, s, fs):
        prods = []
        for c in range(2):
            l, m = a[pair * 2 + c], b[pair * 2 + c]
            lr, li, mr, mi = l[:, :HALF], l[:, HALF:], m[:, :HALF], m[:, HALF:]
            if conj:
                prods.append(jnp.concatenate([lr * mr + li * mi, lr * mi - li * mr], 1))
            else:
                prods.append(jnp.concatenate([lr * mr - li * mi, lr * mi + li * mr], 1))
        d = dot3(split(jnp.concatenate(prods, 0)), (g2h[...], g2l[...]))
        tc, ts = tr[...], ti[...]
        turned = []
        for c in range(2):
            dr, di = d[c * HALF : (c + 1) * HALF, :HALF], d[c * HALF : (c + 1) * HALF, HALF:]
            turned.append(jnp.concatenate([dr * tc + di * ts, di * tc - dr * ts], 0))
        out = dot3((g1h[...], g1l[...]), split(jnp.concatenate(turned, 1)))
        for c in range(2):
            for h in range(2):
                for z in range(2):
                    start = (h * 2 + z) * PLANE
                    s[pl.ds(z * BLOCK + fs * 4 + c * 2 + h, PLANE, stride=TILE), :] = out[
                        start : start + PLANE, c * HALF : (c + 1) * HALF
                    ]

    def take(r, fs, h):
        parts = [r[pl.ds(fs * 4 + c * 2 + h, 2 * PLANE, stride=TILE), :] for c in range(2)]
        return jnp.concatenate(parts, 0).T

    partners = (
        {"ctx": yx * 4 + mz * 2 + 1 - core},
        {"ctx": (y * 4 + x + 1 - 2 * (x % 2)) * 4 + mz * 2 + core},
        {"ctx": (y * 4 + (x + 2) % 4) * 4 + mz * 2 + core},
        {"ctx": ((y + 1 - 2 * (y % 2)) * 4 + x) * 4 + mz * 2 + core},
        {"ctx": (((y + 2) % 4) * 4 + x) * 4 + mz * 2 + core},
        z_device,
    )

    def skip_copy(i):
        return pltpu.make_async_remote_copy(
            src_ref=skip_send.at[i], dst_ref=skip_recv.at[i], send_sem=sk_send.at[i], recv_sem=sk_recv.at[i],
            device_id=partners[i], device_id_type=MESH,
        )

    def skip_step(i):
        skip_copy(i).wait_recv()
        total = skip_send[i] + skip_recv[i]
        if i + 1 < len(partners):
            skip_send[i + 1] = total
            skip_copy(i + 1).start()
        else:
            gs[...] = jnp.sum(total, axis=0, keepdims=True) * (1.0 / HALF)

    for i in range(3):
        loads[i].wait()
    put_inputs(sa1, 0)
    pl.semaphore_wait(barrier, PLANE)
    z_first(0, sa1, ea1, ra1)
    for i in range(3, 5):
        loads[i].wait()
    put_grad(sa2)
    z_first(1, sa2, ea2, ra2)
    put_inputs(sa3, 1)
    z_first(2, sa3, ea3, ra3)
    total = jnp.zeros((TILE, 2 * HALF), F32)
    for i in range(4):
        part = slice(i * 64, (i + 1) * 64)
        prod = (k[part, :].astype(F32) * v[part, :].astype(F32)) * (q[part, :].astype(F32) * cot[part, :].astype(F32))
        total = total + jnp.sum(prod.reshape(8, TILE, 2 * HALF), axis=0)
    skip_send[0] = total
    skip_copy(0).start()
    for i in range(5, len(loads)):
        loads[i].wait()
    for table, high, low in ((f1, f1h, f1l), (f2, f2h, f2l), (g2, g2h, g2l), (g1, g1h, g1l)):
        high[...], low[...] = split(table[...])

    forward(0, sa1, ea1, ra1)
    skip_step(0)
    arrived(0, ra1)
    forward_pair(ra1, 0, spec_u, 0)
    forward_pair(ra1, 1, spec_h, 0)
    inverse_pair(spec_u, spec_h, 0, False, sb2, 0)
    forward(1, sa2, ea2, ra2)
    skip_step(1)
    arrived(1, ra2)
    forward_pair(ra2, 0, spec_g, 0)
    inverse_pair(spec_h, spec_g, 0, True, sb1, 0)
    inverse_pair(spec_u, spec_g, 0, True, sb1, 1)
    z_first(3, sb1, eb1, rb1)
    forward_pair(ra2, 1, spec_g, 1)
    forward(2, sa3, ea3, ra3)
    skip_step(2)
    arrived(2, ra3)
    forward_pair(ra3, 0, spec_u, 1)
    forward_pair(ra3, 1, spec_h, 1)
    inverse_pair(spec_u, spec_h, 1, False, sb2, 1)
    z_first(4, sb2, eb2, rb2)
    skip_step(3)
    inverse_pair(spec_h, spec_g, 1, True, sb3, 0)
    inverse_pair(spec_u, spec_g, 1, True, sb3, 1)
    plane_sends(sb3, oz * BLOCK, eb3, me * TILE, fwd_send.at[5], mid_recv)
    plane_sends(sb3, mz * BLOCK, rb3, (mz * PLANE + me) * TILE, own_send.at[5], plane_recv.at[5])
    skip_step(4)
    forward(3, sb1, eb1, rb1)
    wait_rows(eb3, BLOCK - TILE, mid_recv)
    last = pltpu.make_async_remote_copy(
        src_ref=eb3, dst_ref=rb3.at[rows(mz * BLOCK, BLOCK)], send_sem=z_send.at[5, 0], recv_sem=z_recv.at[5, 0],
        device_id=z_device, device_id_type=MESH,
    )
    last.start()
    skip_step(5)

    def finish_grad(r, pair):
        cols = slice(pair * HALF, (pair + 1) * HALF)
        bias = skip[:, cols]
        for h in range(2):
            at = slice(h * HALF, (h + 1) * HALF)
            grad = take(r, 0, h) + bias * (piece(q, h, pair) * piece(cot, h, pair))
            gk[at, cols] = (grad * piece(v, h, pair)).astype(BF16)
            gv[at, cols] = (grad * piece(k, h, pair)).astype(BF16)
            gt[at, cols] = take(r, 1, h) * (1.0 / HALF)

    def finish_mixed(r):
        for pair in range(2):
            cols = slice(pair * HALF, (pair + 1) * HALF)
            bias = skip[:, cols]
            for h in range(2):
                at = slice(h * HALF, (h + 1) * HALF)
                mixed = take(r, pair, h) + bias * (piece(k, h, pair) * piece(v, h, pair))
                gated[at, cols] = (piece(q, h, pair) * mixed).astype(BF16)
                gq[at, cols] = (piece(cot, h, pair) * mixed).astype(BF16)

    stores = [
        pltpu.make_async_copy(s, t, store_sem.at[i])
        for i, (s, t) in enumerate(
            zip((gated, gq, gs, gk, gv, gt), (gated_out, gq_out, gs_out, gk_out, gv_out, gt_out))
        )
    ]
    arrived(3, rb1)
    finish_grad(rb1, 0)
    forward(4, sb2, eb2, rb2)
    arrived(4, rb2)
    finish_mixed(rb2)
    for store in stores[:3]:
        store.start()
    wait_rows(rb3, BLOCK - TILE, plane_recv.at[5])
    for i, (s, e, r) in enumerate(
        ((sa1, ea1, ra1), (sa2, ea2, ra2), (sa3, ea3, ra3), (sb1, eb1, rb1), (sb2, eb2, rb2))
    ):
        drain(i, s, e, r)
    wait_rows(rb3, BLOCK - TILE, own_send.at[5])
    wait_rows(rb3, BLOCK - TILE, fwd_send.at[5])
    for i in range(len(partners)):
        skip_copy(i).wait_send()
    last.wait()
    finish_grad(rb3, 1)
    for store in stores[3:]:
        store.start()
    for store in stores:
        store.wait()


def shards(query_proj, key_proj, value_proj, filter_taps, skip_bias, cotangent):
    consts = [jnp.asarray(t) for t in tables()]
    shape = query_proj.shape
    args = (query_proj, key_proj, value_proj, filter_taps, skip_bias.reshape(1, -1), cotangent, *consts)
    outs = [jax.ShapeDtypeStruct(shape, BF16)] * 4 + [
        jax.ShapeDtypeStruct(shape, F32),
        jax.ShapeDtypeStruct((1, shape[1]), F32),
    ]
    anywhere = pl.BlockSpec(memory_space=pl.ANY)
    vmem = lambda *s: pltpu.VMEM(s, F32)
    dma = pltpu.SemaphoreType.DMA
    results = pl.pallas_call(
        kernel,
        out_shape=outs,
        in_specs=[anywhere] * len(args),
        out_specs=[anywhere] * len(outs),
        scratch_shapes=[pltpu.VMEM(a.shape, a.dtype) for a in args]
        + [pltpu.VMEM(o.shape, o.dtype) for o in outs]
        + [vmem(ROWS, HALF)] * 6
        + [vmem(BLOCK, HALF)] * 6
        + [vmem(ROWS, HALF)] * 6
        + [vmem(4, HALF, 2 * HALF)] * 3
        + [vmem(6, TILE, 2 * HALF)] * 2
        + [pltpu.VMEM(s, BF16) for s in ((256, 128), (256, 256), (128, 256), (256, 256)) for _ in range(2)]
        + [dma((12,)), dma((6,)), dma((6, 4)), dma((6, 4)), dma((6,)), dma((6,)), dma((6,)), dma, dma((6,)), dma((6,))],
        compiler_params=pltpu.CompilerParams(
            collective_id=0, has_side_effects=True, vmem_limit_bytes=56 * 1024 * 1024
        ),
        name="long_conv",
    )(*args)
    gated, grad_query, grad_key, grad_value, grad_taps, grad_skip = results
    return gated, grad_query, grad_key, grad_value, grad_taps, grad_skip.reshape(-1)


def solution(mesh):
    s = P("ctx", "tp")
    return jax.shard_map(
        shards, mesh=mesh, in_specs=(s, s, s, s, P("tp"), s), out_specs=(s, s, s, s, s, P("tp")), check_vma=False
    )
```

```python
import math

import jax
import jax.numpy as jnp
import numpy as np
from jax import lax
from jax.experimental import pallas as pl
from jax.experimental.pallas import tpu as pltpu
from jax.sharding import PartitionSpec as P

MESH = pl.DeviceIdType.MESH
F32 = jnp.float32
BF16 = jnp.bfloat16
HALF = 128
PLANE = 32
TILE = 8
OWNERS = 2 * PLANE
UNIT = 6
MESSAGE = 4 * UNIT
ROWS = OWNERS * MESSAGE


def tables():
    half, z, source = np.meshgrid(np.arange(2), np.arange(2), np.arange(PLANE), indexing="ij")
    block = (source // 2) * 4 + z * 2 + source % 2
    n1 = (block * 2 + half).reshape(-1)
    k1 = np.arange(HALF) + 0.5
    n2 = np.arange(HALF)
    period = 2 * HALF * HALF
    first = 2 * np.pi * np.outer(k1, n1) / (2 * HALF)
    twist = 2 * np.pi * np.outer(k1, n2) / period
    second = 2 * np.pi * np.outer(n2, np.arange(HALF)) / HALF
    c2, s2 = np.cos(second), np.sin(second)
    f1 = np.concatenate([np.cos(first), -np.sin(first)], 0)
    f2 = np.block([[c2, -s2], [s2, c2]])
    g2 = np.block([[c2, s2], [-s2, c2]])
    g1 = np.concatenate([np.cos(first).T, -np.sin(first).T], 1) * (2 / period)
    return [t.astype(np.float32) for t in (f1, f2, g1, g2, np.cos(twist), -np.sin(twist))]


def split(x):
    high = x.astype(BF16)
    return high, (x - high.astype(F32)).astype(BF16)


def dot(a, b):
    return jnp.dot(a, b, preferred_element_type=F32)


def dot3(a, b):
    return dot(a[0], b[0]) + (dot(a[0], b[1]) + dot(a[1], b[0]))


def kernel(
    q_in, k_in, v_in, taps_in, skip_in, cot_in,
    f1_in, f2_in, g1_in, g2_in, tr_in, ti_in,
    gated_out, gq_out, gk_out, gv_out, gt_out, gs_out,
    q, k, v, taps, skip, cot,
    f1, f2, g1, g2, tr, ti,
    gated, gq, gk, gv, gt, gs,
    sa, sb, ra, rb,
    skip_send, skip_recv, f1h, f1l, f2h, f2l, g1h, g1l, g2h, g2l,
    load_sem, store_sem, send_sem, recv_sem, sk_send, sk_recv,
):
    ctx = lax.axis_index("ctx")
    core, mz, yx = ctx % 2, (ctx // 2) % 2, ctx // 4
    oz = 1 - mz
    me = yx * 2 + core
    yblk, m8 = me // 8, me % 8
    x, y = yx % 4, yx // 4

    def device(z, p):
        return {"ctx": (p // 2) * 4 + z * 2 + p % 2}

    def peer(dy, t):
        a = 2 + 3 * (t // 2)
        dx = jnp.where(t >= 4, 3 - a % 4, a % 4)
        return ((y + dy) % 4 * 4 + (x + dx) % 4) * 2 + (core + 1 - t % 2) % 2

    def to_others(action):
        for z in (oz, mz):
            for dy in (2, 1, 3, 0):

                def body(t, carry, z=z, dy=dy):
                    action(z, peer(dy, t))
                    return carry

                lax.fori_loop(0, 7 if z is mz and dy == 0 else 8, body, 0)

    z_device = {"ctx": yx * 4 + oz * 2 + core}

    def part(owner, c):
        return pl.ds(pl.multiple_of(owner * MESSAGE, TILE) + c * UNIT, UNIT)

    barrier = pltpu.get_barrier_semaphore()

    def greet(z, p):
        pl.semaphore_signal(barrier, inc=1, device_id=device(z, p), device_id_type=MESH)

    sources = (k_in, v_in, taps_in, q_in, cot_in, f1_in, f2_in, g2_in, g1_in, tr_in, ti_in, skip_in)
    targets = (k, v, taps, q, cot, f1, f2, g2, g1, tr, ti, skip)
    loads = [pltpu.make_async_copy(s, t, load_sem.at[i]) for i, (s, t) in enumerate(zip(sources, targets))]
    to_others(greet)
    for load in loads:
        load.start()

    def wait_rows(ref, count, sem):
        pltpu.make_async_copy(ref.at[pl.ds(0, count)], ref.at[pl.ds(0, count)], sem).wait()

    def send(i, c, src, dst):
        mine = part(mz * PLANE + me, c)

        def one(z, p):
            pltpu.make_async_remote_copy(
                src_ref=src.at[part(z * PLANE + p, c)],
                dst_ref=dst.at[mine],
                send_sem=send_sem.at[i],
                recv_sem=recv_sem.at[i],
                device_id=device(z, p),
                device_id_type=MESH,
            ).start()

        to_others(one)
        dst[mine, :] = src[mine, :]

    def arrived(i, r):
        wait_rows(r, (OWNERS - 1) * UNIT, recv_sem.at[i])

    def put(s, pair, field, values, h):
        flipped = values.T
        for c in range(2):
            s[pl.ds((pair * 2 + c) * UNIT + field * 2 + h, OWNERS, stride=MESSAGE), :] = flipped[
                c * OWNERS : (c + 1) * OWNERS
            ]

    def piece(ref, h, pair):
        return ref[h * HALF : (h + 1) * HALF, pair * HALF : (pair + 1) * HALF].astype(F32)

    def lay_out(s, pair):
        for h in range(2):
            put(s, pair, 0, piece(k, h, pair) * piece(v, h, pair), h)
            put(s, pair, 1, piece(taps, h, pair), h)
            put(s, pair, 2, piece(q, h, pair) * piece(cot, h, pair), h)

    def series_rows(c, field, h, z):
        return pl.ds(z * PLANE * MESSAGE + c * UNIT + field * 2 + h, PLANE, stride=MESSAGE)

    def transform(c):
        series = []
        for field in range(3):
            parts = [ra[series_rows(c, field, h, z), :] for h in range(2) for z in range(2)]
            series.append(jnp.concatenate(parts, 0))
        a = dot3((f1h[...], f1l[...]), split(jnp.concatenate(series, 1)))
        tc, ts = tr[...], ti[...]
        turned = []
        for field in range(3):
            cols = slice(field * HALF, (field + 1) * HALF)
            ar, ai = a[:HALF, cols], a[HALF:, cols]
            turned.append(jnp.concatenate([ar * tc - ai * ts, ar * ts + ai * tc], 1))
        b = dot3(split(jnp.concatenate(turned, 0)), (f2h[...], f2l[...]))
        (ur, ui), (hr, hi), (gr, gi) = [
            (b[f * HALF : (f + 1) * HALF, :HALF], b[f * HALF : (f + 1) * HALF, HALF:]) for f in range(3)
        ]
        prods = jnp.concatenate(
            [
                jnp.concatenate([ur * hr - ui * hi, ur * hi + ui * hr], 1),
                jnp.concatenate([hr * gr + hi * gi, hr * gi - hi * gr], 1),
                jnp.concatenate([ur * gr + ui * gi, ur * gi - ui * gr], 1),
            ],
            0,
        )
        d = dot3(split(prods), (g2h[...], g2l[...]))
        turned = []
        for field in range(3):
            at = slice(field * HALF, (field + 1) * HALF)
            dr, di = d[at, :HALF], d[at, HALF:]
            turned.append(jnp.concatenate([dr * tc + di * ts, di * tc - dr * ts], 0))
        out = dot3((g1h[...], g1l[...]), split(jnp.concatenate(turned, 1)))
        for field in range(3):
            for h in range(2):
                for z in range(2):
                    start = (h * 2 + z) * PLANE
                    sb[series_rows(c, field, h, z), :] = out[
                        start : start + PLANE, field * HALF : (field + 1) * HALF
                    ]

    def take(pair, field, h):
        parts = [
            rb[pl.ds((pair * 2 + c) * UNIT + field * 2 + h, OWNERS, stride=MESSAGE), :] for c in range(2)
        ]
        return jnp.concatenate(parts, 0).T

    partners = (
        {"ctx": yx * 4 + mz * 2 + 1 - core},
        {"ctx": (y * 4 + x + 1 - 2 * (x % 2)) * 4 + mz * 2 + core},
        {"ctx": (y * 4 + (x + 2) % 4) * 4 + mz * 2 + core},
        {"ctx": ((y + 1 - 2 * (y % 2)) * 4 + x) * 4 + mz * 2 + core},
        {"ctx": (((y + 2) % 4) * 4 + x) * 4 + mz * 2 + core},
        z_device,
    )

    def skip_copy(i):
        return pltpu.make_async_remote_copy(
            src_ref=skip_send.at[i], dst_ref=skip_recv.at[i], send_sem=sk_send.at[i], recv_sem=sk_recv.at[i],
            device_id=partners[i], device_id_type=MESH,
        )

    def skip_step(i):
        skip_copy(i).wait_recv()
        total = skip_send[i] + skip_recv[i]
        if i + 1 < len(partners):
            skip_send[i + 1] = total
            skip_copy(i + 1).start()
        else:
            gs[...] = jnp.sum(total, axis=0, keepdims=True) * (1.0 / HALF)

    for i in range(5):
        loads[i].wait()
    for pair in range(2):
        lay_out(sa, pair)
    pl.semaphore_wait(barrier, OWNERS - 1)
    for c in range(4):
        send(c, c, sa, ra)
    total = jnp.zeros((TILE, 2 * HALF), F32)
    for i in range(4):
        at = slice(i * 64, (i + 1) * 64)
        prod = (k[at, :].astype(F32) * v[at, :].astype(F32)) * (q[at, :].astype(F32) * cot[at, :].astype(F32))
        total = total + jnp.sum(prod.reshape(8, TILE, 2 * HALF), axis=0)
    skip_send[0] = total
    skip_copy(0).start()
    for i in range(5, len(loads)):
        loads[i].wait()
    for table, high, low in ((f1, f1h, f1l), (f2, f2h, f2l), (g2, g2h, g2l), (g1, g1h, g1l)):
        high[...], low[...] = split(table[...])
    skip_step(0)
    for c in range(4):
        arrived(c, ra)
        transform(c)
        send(4 + c, c, sb, rb)
        skip_step(c + 1)

    def finish(pair):
        cols = slice(pair * HALF, (pair + 1) * HALF)
        bias = skip[:, cols]
        for h in range(2):
            at = slice(h * HALF, (h + 1) * HALF)
            qp, kp, vp, cp = [piece(ref, h, pair) for ref in (q, k, v, cot)]
            mixed = take(pair, 0, h) + bias * (kp * vp)
            gated[at, cols] = (qp * mixed).astype(BF16)
            gq[at, cols] = (cp * mixed).astype(BF16)
            grad = take(pair, 1, h) + bias * (qp * cp)
            gk[at, cols] = (grad * vp).astype(BF16)
            gv[at, cols] = (grad * kp).astype(BF16)
            gt[at, cols] = take(pair, 2, h) * (1.0 / HALF)

    stores = [
        pltpu.make_async_copy(s, t, store_sem.at[i])
        for i, (s, t) in enumerate(
            zip((gated, gq, gs, gk, gv, gt), (gated_out, gq_out, gs_out, gk_out, gv_out, gt_out))
        )
    ]
    arrived(4, rb)
    arrived(5, rb)
    finish(0)
    skip_step(5)
    for i in range(8):
        wait_rows(ra, (OWNERS - 1) * UNIT, send_sem.at[i])
    for i in range(len(partners)):
        skip_copy(i).wait_send()
    arrived(6, rb)
    arrived(7, rb)
    finish(1)
    for store in stores:
        store.start()
    for store in stores:
        store.wait()


def hand_on(*refs):
    count = len(refs) // 3
    into, out = refs[-2:]
    reads = [pltpu.make_async_copy(refs[i], refs[2 * count + i], into.at[i]) for i in range(count)]
    writes = [pltpu.make_async_copy(refs[2 * count + i], refs[count + i], out.at[i]) for i in range(count)]
    for read in reads:
        read.start()
    for read, write in zip(reads, writes):
        read.wait()
        write.start()
    for write in writes:
        write.wait()


def shards(query_proj, key_proj, value_proj, filter_taps, skip_bias, cotangent):
    consts = [jnp.asarray(t) for t in tables()]
    shape = query_proj.shape
    args = (query_proj, key_proj, value_proj, filter_taps, skip_bias.reshape(1, -1), cotangent, *consts)
    outs = [jax.ShapeDtypeStruct(shape, BF16)] * 4 + [
        jax.ShapeDtypeStruct(shape, F32),
        jax.ShapeDtypeStruct((1, shape[1]), F32),
    ]
    anywhere = pl.BlockSpec(memory_space=pl.ANY)
    vmem = lambda *s: pltpu.VMEM(s, F32)
    dma = pltpu.SemaphoreType.DMA
    results = pl.pallas_call(
        kernel,
        out_shape=outs,
        in_specs=[anywhere] * len(args),
        out_specs=[anywhere] * len(outs),
        scratch_shapes=[pltpu.VMEM(a.shape, a.dtype) for a in args]
        + [pltpu.VMEM(o.shape, o.dtype) for o in outs]
        + [vmem(ROWS, HALF)] * 4
        + [vmem(6, TILE, 2 * HALF)] * 2
        + [pltpu.VMEM(s, BF16) for s in ((256, 128), (256, 256), (128, 256), (256, 256)) for _ in range(2)]
        + [dma((12,)), dma((6,)), dma((8,)), dma((8,)), dma((6,)), dma((6,))],
        compiler_params=pltpu.CompilerParams(
            collective_id=0, has_side_effects=True, vmem_limit_bytes=56 * 1024 * 1024
        ),
        name="long_conv",
    )(*args)
    gated, grad_query, grad_key, grad_value, grad_taps, grad_skip = pl.pallas_call(
        hand_on,
        out_shape=outs,
        in_specs=[anywhere] * len(outs),
        out_specs=[anywhere] * len(outs),
        scratch_shapes=[pltpu.VMEM(o.shape, o.dtype) for o in outs] + [dma((len(outs),))] * 2,
        compiler_params=pltpu.CompilerParams(vmem_limit_bytes=56 * 1024 * 1024),
        name="hand_on",
    )(*results)
    return gated, grad_query, grad_key, grad_value, grad_taps, grad_skip.reshape(-1)


def solution(mesh):
    s = P("ctx", "tp")
    return jax.shard_map(
        shards, mesh=mesh, in_specs=(s, s, s, s, P("tp"), s), out_specs=(s, s, s, s, s, P("tp")), check_vma=False
    )
```

```python
import math

import jax
import jax.numpy as jnp
import numpy as np
from jax import lax
from jax.experimental import pallas as pl
from jax.experimental.pallas import tpu as pltpu
from jax.sharding import PartitionSpec as P

MESH = pl.DeviceIdType.MESH
F32 = jnp.float32
BF16 = jnp.bfloat16
HALF = 128
PLANE = 32
TILE = 8
OWNERS = 2 * PLANE
UNIT = 6
FAR_FIRST = (2, 1, 3, 0)
SPAN = OWNERS * TILE
ROWS = 4 * SPAN


def tables():
    half, z, source = np.meshgrid(np.arange(2), np.arange(2), np.arange(PLANE), indexing="ij")
    block = (source // 2) * 4 + z * 2 + source % 2
    n1 = (block * 2 + half).reshape(-1)
    k1 = np.arange(HALF) + 0.5
    n2 = np.arange(HALF)
    period = 2 * HALF * HALF
    first = 2 * np.pi * np.outer(k1, n1) / (2 * HALF)
    twist = 2 * np.pi * np.outer(k1, n2) / period
    second = 2 * np.pi * np.outer(n2, np.arange(HALF)) / HALF
    c2, s2 = np.cos(second), np.sin(second)
    f1 = np.concatenate([np.cos(first), -np.sin(first)], 0)
    f2 = np.block([[c2, -s2], [s2, c2]])
    g2 = np.block([[c2, s2], [-s2, c2]])
    g1 = np.concatenate([np.cos(first).T, -np.sin(first).T], 1) * (2 / period)
    return [t.astype(np.float32) for t in (f1, f2, g1, g2, np.cos(twist), -np.sin(twist))]


def split(x):
    high = x.astype(BF16)
    return high, (x - high.astype(F32)).astype(BF16)


def dot(a, b):
    return jnp.dot(a, b, preferred_element_type=F32)


def dot_left(first, second, x):
    high, low = split(x)
    return dot(first, jnp.concatenate([high, high], 0)) + dot(second, low)


def dot_right(x, high_table, low_table):
    high, low = split(x)
    count = x.shape[0]
    both = dot(jnp.concatenate([high, low], 0), high_table)
    return both[:count] + (both[count:] + dot(high, low_table))


def dot_stacked(both_tables, high_table, x):
    high, low = split(x)
    both = dot(both_tables, high)
    count = high_table.shape[0]
    return both[:count] + (both[count:] + dot(high_table, low))


def kernel(
    q_in, k_in, v_in, taps_in, skip_in, cot_in,
    f1_in, f2_in, g1_in, g2_in, tr_in, ti_in,
    gated_out, gq_out, gk_out, gv_out, gt_out, gs_out,
    q, k, v, taps, skip, cot,
    f1, f2, g1, g2, tr, ti,
    gated, gq, gk, gv, gt, gs,
    sa, sb, ra, rb, ea,
    skip_send, skip_recv, f1h, f1b, f2h, f2l, g1h, g1b, g2h, g2l,
    load_sem, store_sem, send_sem, recv_sem, sk_send, sk_recv, over_send, over_recv, column_sem, core_sem, plane_sem,
):
    ctx = lax.axis_index("ctx")
    core, mz, yx = ctx % 2, (ctx // 2) % 2, ctx // 4
    oz = 1 - mz
    me = yx * 2 + core
    yblk, m8 = me // 8, me % 8
    x, y = yx % 4, yx // 4

    def device(z, p):
        return {"ctx": (p // 2) * 4 + z * 2 + p % 2}

    def peer(dy, t):
        a = 2 + 3 * (t // 2)
        dx = jnp.where(t >= 4, 3 - a % 4, a % 4)
        return ((y + dy) % 4 * 4 + (x + dx) % 4) * 2 + (core + 1 - t % 2) % 2

    def to_plane(action, z, self_too=False):
        for dy in FAR_FIRST:

            def body(t, carry, dy=dy):
                action(z, peer(dy, t))
                return carry

            lax.fori_loop(0, 8 if self_too or dy else 7, body, 0)

    def to_others(action):
        to_plane(action, oz, True)
        to_plane(action, mz)

    z_device = {"ctx": yx * 4 + oz * 2 + core}
    core_device = {"ctx": yx * 4 + mz * 2 + 1 - core}
    row = [{"ctx": (y * 4 + (x + d) % 4) * 4 + mz * 2 + core} for d in (2, 1, 3)]
    column = [{"ctx": ((y + d) % 4 * 4 + x) * 4 + mz * 2 + core} for d in (2, 1, 3)]

    def signal(sem, devices):
        for target in devices:
            pl.semaphore_signal(sem, inc=1, device_id=target, device_id_type=MESH)

    def part(owner, c):
        return pl.ds(pl.multiple_of(c * SPAN + owner * TILE, TILE), UNIT)

    barrier = pltpu.get_barrier_semaphore()

    sources = (k_in, v_in, taps_in, q_in, cot_in, f1_in, f2_in, g2_in, g1_in, tr_in, ti_in, skip_in)
    targets = (k, v, taps, q, cot, f1, f2, g2, g1, tr, ti, skip)
    loads = [pltpu.make_async_copy(s, t, load_sem.at[i]) for i, (s, t) in enumerate(zip(sources, targets))]
    for load in loads[:5]:
        load.start()
    signal(barrier, [z_device, *column, *row, core_device])
    for load in loads[5:]:
        load.start()

    def wait_rows(ref, count, sem):
        pltpu.make_async_copy(ref.at[pl.ds(0, count)], ref.at[pl.ds(0, count)], sem).wait()

    def give(src, at, dst, i, c, z, p, source):
        pltpu.make_async_remote_copy(
            src_ref=src.at[at],
            dst_ref=dst.at[part(source * PLANE + me, c)],
            send_sem=send_sem.at[i],
            recv_sem=recv_sem.at[i],
            device_id=device(z, p),
            device_id_type=MESH,
        ).start()

    def keep(src, at, dst, c, source):
        dst[part(source * PLANE + me, c), :] = src[at, :]

    def parked(p, c):
        return pl.ds(pl.multiple_of((c * PLANE + p) * TILE, TILE), UNIT)

    def cross(c):
        for k, dy in enumerate(FAR_FIRST):

            def one(t, carry, k=k, dy=dy):
                p = peer(dy, t)
                pltpu.make_async_remote_copy(
                    src_ref=sa.at[part(oz * PLANE + p, c)],
                    dst_ref=ea.at[parked(p, c)],
                    send_sem=over_send.at[c],
                    recv_sem=over_recv.at[c, k],
                    device_id=z_device,
                    device_id_type=MESH,
                ).start()
                return carry

            lax.fori_loop(0, 8, one, 0)

    def own_plane(c):
        to_plane(lambda z, p: give(sa, part(z * PLANE + p, c), ra, c, c, z, p, mz), mz)
        keep(sa, part(mz * PLANE + me, c), ra, c, mz)

    def hand_over(c):
        for k, dy in enumerate(FAR_FIRST):
            wait_rows(ea, 8 * UNIT, over_recv.at[c, k])

            def one(t, carry, dy=dy):
                p = peer(dy, t)
                give(ea, parked(p, c), ra, c, c, mz, p, oz)
                return carry

            lax.fori_loop(0, 8 if dy else 7, one, 0)
        keep(ea, parked(me, c), ra, c, oz)

    def back(c):
        to_others(lambda z, p: give(sb, part(z * PLANE + p, c), rb, 4 + c, c, z, p, mz))
        keep(sb, part(mz * PLANE + me, c), rb, c, mz)

    def moved(i, sem):
        wait_rows(ra, (OWNERS - 1 - (i < 4)) * UNIT, sem.at[i])

    def put(s, pair, field, values, h):
        flipped = values.T
        for c in range(2):
            s[pl.ds((pair * 2 + c) * SPAN + field * 2 + h, OWNERS, stride=TILE), :] = flipped[
                c * OWNERS : (c + 1) * OWNERS
            ]

    def piece(ref, h, pair):
        return ref[h * HALF : (h + 1) * HALF, pair * HALF : (pair + 1) * HALF].astype(F32)

    def lay_out(s, pair):
        for h in range(2):
            put(s, pair, 0, piece(k, h, pair) * piece(v, h, pair), h)
            put(s, pair, 1, piece(taps, h, pair), h)
            put(s, pair, 2, piece(q, h, pair) * piece(cot, h, pair), h)

    def series_rows(c, field, h, z):
        return pl.ds(c * SPAN + z * PLANE * TILE + field * 2 + h, PLANE, stride=TILE)

    def transform(c):
        series = []
        for field in range(3):
            parts = [ra[series_rows(c, field, h, z), :] for h in range(2) for z in range(2)]
            series.append(jnp.concatenate(parts, 0))
        a = dot_left(f1b[...], f1h[...], jnp.concatenate(series, 1))
        tc, ts = tr[...], ti[...]
        turned = []
        for field in range(3):
            cols = slice(field * HALF, (field + 1) * HALF)
            ar, ai = a[:HALF, cols], a[HALF:, cols]
            turned.append(jnp.concatenate([ar * tc - ai * ts, ar * ts + ai * tc], 1))
        b = dot_right(jnp.concatenate(turned, 0), f2h[...], f2l[...])
        (ur, ui), (hr, hi), (gr, gi) = [
            (b[f * HALF : (f + 1) * HALF, :HALF], b[f * HALF : (f + 1) * HALF, HALF:]) for f in range(3)
        ]
        prods = jnp.concatenate(
            [
                jnp.concatenate([ur * hr - ui * hi, ur * hi + ui * hr], 1),
                jnp.concatenate([hr * gr + hi * gi, hr * gi - hi * gr], 1),
                jnp.concatenate([ur * gr + ui * gi, ur * gi - ui * gr], 1),
            ],
            0,
        )
        d = dot_right(prods, g2h[...], g2l[...])
        turned = []
        for field in range(3):
            at = slice(field * HALF, (field + 1) * HALF)
            dr, di = d[at, :HALF], d[at, HALF:]
            turned.append(jnp.concatenate([dr * tc + di * ts, di * tc - dr * ts], 0))
        out = dot_stacked(g1b[...], g1h[...], jnp.concatenate(turned, 1))
        for field in range(3):
            for h in range(2):
                for z in range(2):
                    start = (h * 2 + z) * PLANE
                    sb[series_rows(c, field, h, z), :] = out[
                        start : start + PLANE, field * HALF : (field + 1) * HALF
                    ]

    def take(pair, field, h):
        parts = [
            rb[pl.ds((pair * 2 + c) * SPAN + field * 2 + h, OWNERS, stride=TILE), :] for c in range(2)
        ]
        return jnp.concatenate(parts, 0).T

    partners = (
        {"ctx": yx * 4 + mz * 2 + 1 - core},
        {"ctx": (y * 4 + x + 1 - 2 * (x % 2)) * 4 + mz * 2 + core},
        {"ctx": (y * 4 + (x + 2) % 4) * 4 + mz * 2 + core},
        {"ctx": ((y + 1 - 2 * (y % 2)) * 4 + x) * 4 + mz * 2 + core},
        {"ctx": (((y + 2) % 4) * 4 + x) * 4 + mz * 2 + core},
        z_device,
    )

    def skip_copy(i):
        return pltpu.make_async_remote_copy(
            src_ref=skip_send.at[i], dst_ref=skip_recv.at[i], send_sem=sk_send.at[i], recv_sem=sk_recv.at[i],
            device_id=partners[i], device_id_type=MESH,
        )

    def skip_step(i):
        skip_copy(i).wait_recv()
        total = skip_send[i] + skip_recv[i]
        if i + 1 < len(partners):
            skip_send[i + 1] = total
            skip_copy(i + 1).start()
        else:
            gs[...] = jnp.sum(total, axis=0, keepdims=True) * (1.0 / HALF)

    for i in range(5):
        loads[i].wait()
    lay_out(sa, 0)
    pl.semaphore_wait(barrier, 8)
    cross(0)
    cross(1)
    signal(column_sem, column)
    lay_out(sa, 1)
    cross(2)
    cross(3)
    pl.semaphore_wait(column_sem, 3)
    signal(core_sem, [core_device])
    pl.semaphore_wait(core_sem, 1)
    signal(plane_sem, [z_device])
    for c in range(4):
        own_plane(c)
    total = jnp.zeros((TILE, 2 * HALF), F32)
    for i in range(4):
        at = slice(i * 64, (i + 1) * 64)
        prod = (k[at, :].astype(F32) * v[at, :].astype(F32)) * (q[at, :].astype(F32) * cot[at, :].astype(F32))
        total = total + jnp.sum(prod.reshape(8, TILE, 2 * HALF), axis=0)
    skip_send[0] = total
    skip_copy(0).start()
    for i in range(5, len(loads)):
        loads[i].wait()
    for table, high, low in ((f2, f2h, f2l), (g2, g2h, g2l)):
        high[...], low[...] = split(table[...])
    high, low = split(f1[...])
    f1h[...], f1b[...] = high, jnp.concatenate([high, low], 1)
    high, low = split(g1[...])
    g1h[...], g1b[...] = high, jnp.concatenate([high, low], 0)
    skip_step(0)
    hand_over(0)
    for c in range(4):
        if c < 3:
            hand_over(c + 1)
        moved(c, recv_sem)
        transform(c)
        if c == 0:
            pl.semaphore_wait(plane_sem, 1)
        back(c)
        skip_step(c + 1)

    def finish(pair):
        cols = slice(pair * HALF, (pair + 1) * HALF)
        bias = skip[:, cols]
        for h in range(2):
            at = slice(h * HALF, (h + 1) * HALF)
            qp, kp, vp, cp = [piece(ref, h, pair) for ref in (q, k, v, cot)]
            mixed = take(pair, 0, h) + bias * (kp * vp)
            gated[at, cols] = (qp * mixed).astype(BF16)
            gq[at, cols] = (cp * mixed).astype(BF16)
            grad = take(pair, 1, h) + bias * (qp * cp)
            gk[at, cols] = (grad * vp).astype(BF16)
            gv[at, cols] = (grad * kp).astype(BF16)
            gt[at, cols] = take(pair, 2, h) * (1.0 / HALF)

    stores = [
        pltpu.make_async_copy(s, t, store_sem.at[i])
        for i, (s, t) in enumerate(
            zip((gated, gq, gs, gk, gv, gt), (gated_out, gq_out, gs_out, gk_out, gv_out, gt_out))
        )
    ]
    moved(4, recv_sem)
    moved(5, recv_sem)
    finish(0)
    skip_step(5)
    for c in range(4):
        wait_rows(ea, PLANE * UNIT, over_send.at[c])
    for i in range(8):
        moved(i, send_sem)
    for i in range(len(partners)):
        skip_copy(i).wait_send()
    moved(6, recv_sem)
    moved(7, recv_sem)
    finish(1)
    for store in stores:
        store.start()
    for store in stores:
        store.wait()


def hand_on(*refs):
    count = len(refs) // 3
    into, out = refs[-2:]
    reads = [pltpu.make_async_copy(refs[i], refs[2 * count + i], into.at[i]) for i in range(count)]
    writes = [pltpu.make_async_copy(refs[2 * count + i], refs[count + i], out.at[i]) for i in range(count)]
    for read in reads:
        read.start()
    for read, write in zip(reads, writes):
        read.wait()
        write.start()
    for write in writes:
        write.wait()


def shards(query_proj, key_proj, value_proj, filter_taps, skip_bias, cotangent):
    consts = [jnp.asarray(t) for t in tables()]
    shape = query_proj.shape
    args = (query_proj, key_proj, value_proj, filter_taps, skip_bias.reshape(1, -1), cotangent, *consts)
    outs = [jax.ShapeDtypeStruct(shape, BF16)] * 4 + [
        jax.ShapeDtypeStruct(shape, F32),
        jax.ShapeDtypeStruct((1, shape[1]), F32),
    ]
    anywhere = pl.BlockSpec(memory_space=pl.ANY)
    vmem = lambda *s: pltpu.VMEM(s, F32)
    dma = pltpu.SemaphoreType.DMA
    results = pl.pallas_call(
        kernel,
        out_shape=outs,
        in_specs=[anywhere] * len(args),
        out_specs=[anywhere] * len(outs),
        scratch_shapes=[pltpu.VMEM(a.shape, a.dtype) for a in args]
        + [pltpu.VMEM(o.shape, o.dtype) for o in outs]
        + [vmem(ROWS, HALF)] * 4
        + [vmem(4 * PLANE * TILE, HALF)]
        + [vmem(6, TILE, 2 * HALF)] * 2
        + [
            pltpu.VMEM(s, BF16)
            for s in ((256, 128), (256, 256), (256, 256), (256, 256), (128, 256), (256, 256), (256, 256), (256, 256))
        ]
        + [dma((12,)), dma((6,)), dma((8,)), dma((8,)), dma((6,)), dma((6,)), dma((4,)), dma((4, 4))]
        + [pltpu.SemaphoreType.REGULAR] * 3,
        compiler_params=pltpu.CompilerParams(
            collective_id=0, has_side_effects=True, vmem_limit_bytes=56 * 1024 * 1024
        ),
        name="long_conv",
    )(*args)
    gated, grad_query, grad_key, grad_value, grad_taps, grad_skip = pl.pallas_call(
        hand_on,
        out_shape=outs,
        in_specs=[anywhere] * len(outs),
        out_specs=[anywhere] * len(outs),
        scratch_shapes=[pltpu.VMEM(o.shape, o.dtype) for o in outs] + [dma((len(outs),))] * 2,
        compiler_params=pltpu.CompilerParams(vmem_limit_bytes=56 * 1024 * 1024),
        name="hand_on",
    )(*results)
    return gated, grad_query, grad_key, grad_value, grad_taps, grad_skip.reshape(-1)


def solution(mesh):
    s = P("ctx", "tp")
    return jax.shard_map(
        shards, mesh=mesh, in_specs=(s, s, s, s, P("tp"), s), out_specs=(s, s, s, s, s, P("tp")), check_vma=False
    )
```

```python
import math

import jax
import jax.numpy as jnp
import numpy as np
from jax import lax
from jax.experimental import pallas as pl
from jax.experimental.pallas import tpu as pltpu
from jax.sharding import PartitionSpec as P

MESH = pl.DeviceIdType.MESH
F32 = jnp.float32
BF16 = jnp.bfloat16
HALF = 128
PLANE = 32
TILE = 8
OWNERS = 2 * PLANE
UNIT = 6
FAR_FIRST = (2, 1, 3, 0)
SPAN = OWNERS * TILE
ROWS = 4 * SPAN


def tables():
    half, z, source = np.meshgrid(np.arange(2), np.arange(2), np.arange(PLANE), indexing="ij")
    block = (source // 2) * 4 + z * 2 + source % 2
    n1 = (block * 2 + half).reshape(-1)
    k1 = np.arange(HALF) + 0.5
    n2 = np.arange(HALF)
    period = 2 * HALF * HALF
    first = 2 * np.pi * np.outer(k1, n1) / (2 * HALF)
    twist = 2 * np.pi * np.outer(k1, n2) / period
    second = 2 * np.pi * np.outer(n2, np.arange(HALF)) / HALF
    c2, s2 = np.cos(second), np.sin(second)
    f1 = np.concatenate([np.cos(first), -np.sin(first)], 0)
    f2 = np.block([[c2, -s2], [s2, c2]])
    g2 = np.block([[c2, s2], [-s2, c2]])
    g1 = np.concatenate([np.cos(first).T, -np.sin(first).T], 1) * (2 / period)
    return [t.astype(np.float32) for t in (f1, f2, g1, g2, np.cos(twist), -np.sin(twist))]


def split(x):
    high = x.astype(BF16)
    return high, (x - high.astype(F32)).astype(BF16)


def dot(a, b):
    return jnp.dot(a, b, preferred_element_type=F32)


def dot_left(first, second, x):
    high, low = split(x)
    return dot(first, jnp.concatenate([high, high], 0)) + dot(second, low)


def dot_right(x, high_table, low_table):
    high, low = split(x)
    count = x.shape[0]
    both = dot(jnp.concatenate([high, low], 0), high_table)
    return both[:count] + (both[count:] + dot(high, low_table))


def dot_stacked(both_tables, high_table, x):
    high, low = split(x)
    both = dot(both_tables, high)
    count = high_table.shape[0]
    return both[:count] + (both[count:] + dot(high_table, low))


def kernel(
    q_in, k_in, v_in, taps_in, skip_in, cot_in,
    f1_in, f2_in, g1_in, g2_in, tr_in, ti_in,
    gated, gq, gk, gv, gt, gs,
    q, k, v, taps, skip, cot,
    f1, f2, g1, g2, tr, ti,
    sa, sb, ra, rb, ea,
    skip_send, skip_recv, f1h, f1b, f2h, f2l, g1h, g1b, g2h, g2l,
    load_sem, send_sem, recv_sem, sk_send, sk_recv, over_send, over_recv, column_sem, core_sem, plane_sem,
):
    ctx = lax.axis_index("ctx")
    core, mz, yx = ctx % 2, (ctx // 2) % 2, ctx // 4
    oz = 1 - mz
    me = yx * 2 + core
    yblk, m8 = me // 8, me % 8
    x, y = yx % 4, yx // 4

    def device(z, p):
        return {"ctx": (p // 2) * 4 + z * 2 + p % 2}

    def peer(dy, t):
        a = 2 + 3 * (t // 2)
        dx = jnp.where(t >= 4, 3 - a % 4, a % 4)
        return ((y + dy) % 4 * 4 + (x + dx) % 4) * 2 + (core + 1 - t % 2) % 2

    def to_plane(action, z, self_too=False):
        for dy in FAR_FIRST:

            def body(t, carry, dy=dy):
                action(z, peer(dy, t))
                return carry

            lax.fori_loop(0, 8 if self_too or dy else 7, body, 0)

    def to_others(action):
        to_plane(action, oz, True)
        to_plane(action, mz)

    z_device = {"ctx": yx * 4 + oz * 2 + core}
    core_device = {"ctx": yx * 4 + mz * 2 + 1 - core}
    row = [{"ctx": (y * 4 + (x + d) % 4) * 4 + mz * 2 + core} for d in (2, 1, 3)]
    column = [{"ctx": ((y + d) % 4 * 4 + x) * 4 + mz * 2 + core} for d in (2, 1, 3)]

    def signal(sem, devices):
        for target in devices:
            pl.semaphore_signal(sem, inc=1, device_id=target, device_id_type=MESH)

    def part(owner, c):
        return pl.ds(pl.multiple_of(c * SPAN + owner * TILE, TILE), UNIT)

    barrier = pltpu.get_barrier_semaphore()

    sources = (k_in, v_in, taps_in, q_in, cot_in, f1_in, f2_in, g2_in, g1_in, tr_in, ti_in, skip_in)
    targets = (k, v, taps, q, cot, f1, f2, g2, g1, tr, ti, skip)
    loads = [pltpu.make_async_copy(s, t, load_sem.at[i]) for i, (s, t) in enumerate(zip(sources, targets))]
    for load in loads[:5]:
        load.start()
    signal(barrier, [z_device, *column, *row, core_device])
    for load in loads[5:]:
        load.start()

    def wait_rows(ref, count, sem):
        pltpu.make_async_copy(ref.at[pl.ds(0, count)], ref.at[pl.ds(0, count)], sem).wait()

    def give(src, at, dst, i, c, z, p, source):
        pltpu.make_async_remote_copy(
            src_ref=src.at[at],
            dst_ref=dst.at[part(source * PLANE + me, c)],
            send_sem=send_sem.at[i],
            recv_sem=recv_sem.at[i],
            device_id=device(z, p),
            device_id_type=MESH,
        ).start()

    def keep(src, at, dst, c, source):
        dst[part(source * PLANE + me, c), :] = src[at, :]

    def parked(p, c):
        return pl.ds(pl.multiple_of((c * PLANE + p) * TILE, TILE), UNIT)

    def cross(c):
        for k, dy in enumerate(FAR_FIRST):

            def one(t, carry, k=k, dy=dy):
                p = peer(dy, t)
                pltpu.make_async_remote_copy(
                    src_ref=sa.at[part(oz * PLANE + p, c)],
                    dst_ref=ea.at[parked(p, c)],
                    send_sem=over_send.at[c],
                    recv_sem=over_recv.at[c, k],
                    device_id=z_device,
                    device_id_type=MESH,
                ).start()
                return carry

            lax.fori_loop(0, 8, one, 0)

    def own_plane(c):
        to_plane(lambda z, p: give(sa, part(z * PLANE + p, c), ra, c, c, z, p, mz), mz)
        keep(sa, part(mz * PLANE + me, c), ra, c, mz)

    def hand_over(c):
        for k, dy in enumerate(FAR_FIRST):
            wait_rows(ea, 8 * UNIT, over_recv.at[c, k])

            def one(t, carry, dy=dy):
                p = peer(dy, t)
                give(ea, parked(p, c), ra, c, c, mz, p, oz)
                return carry

            lax.fori_loop(0, 8 if dy else 7, one, 0)
        keep(ea, parked(me, c), ra, c, oz)

    def direct(src, dst, i, c):
        to_others(lambda z, p: give(src, part(z * PLANE + p, c), dst, i, c, z, p, mz))
        keep(src, part(mz * PLANE + me, c), dst, c, mz)

    def moved(i, sem):
        count = 2 * (PLANE - 1) if i < 3 else OWNERS - 1
        wait_rows(ra, count * UNIT, sem.at[i])

    def put(s, pair, field, values, h):
        flipped = values.T
        for c in range(2):
            s[pl.ds((pair * 2 + c) * SPAN + field * 2 + h, OWNERS, stride=TILE), :] = flipped[
                c * OWNERS : (c + 1) * OWNERS
            ]

    def piece(ref, h, pair):
        return ref[h * HALF : (h + 1) * HALF, pair * HALF : (pair + 1) * HALF].astype(F32)

    def lay_out(s, pair):
        for h in range(2):
            put(s, pair, 0, piece(k, h, pair) * piece(v, h, pair), h)
            put(s, pair, 1, piece(taps, h, pair), h)
            put(s, pair, 2, piece(q, h, pair) * piece(cot, h, pair), h)

    def series_rows(c, field, h, z):
        return pl.ds(c * SPAN + z * PLANE * TILE + field * 2 + h, PLANE, stride=TILE)

    def transform(c):
        series = []
        for field in range(3):
            parts = [ra[series_rows(c, field, h, z), :] for h in range(2) for z in range(2)]
            series.append(jnp.concatenate(parts, 0))
        a = dot_left(f1b[...], f1h[...], jnp.concatenate(series, 1))
        tc, ts = tr[...], ti[...]
        turned = []
        for field in range(3):
            cols = slice(field * HALF, (field + 1) * HALF)
            ar, ai = a[:HALF, cols], a[HALF:, cols]
            turned.append(jnp.concatenate([ar * tc - ai * ts, ar * ts + ai * tc], 1))
        b = dot_right(jnp.concatenate(turned, 0), f2h[...], f2l[...])
        (ur, ui), (hr, hi), (gr, gi) = [
            (b[f * HALF : (f + 1) * HALF, :HALF], b[f * HALF : (f + 1) * HALF, HALF:]) for f in range(3)
        ]
        prods = jnp.concatenate(
            [
                jnp.concatenate([ur * hr - ui * hi, ur * hi + ui * hr], 1),
                jnp.concatenate([hr * gr + hi * gi, hr * gi - hi * gr], 1),
                jnp.concatenate([ur * gr + ui * gi, ur * gi - ui * gr], 1),
            ],
            0,
        )
        d = dot_right(prods, g2h[...], g2l[...])
        turned = []
        for field in range(3):
            at = slice(field * HALF, (field + 1) * HALF)
            dr, di = d[at, :HALF], d[at, HALF:]
            turned.append(jnp.concatenate([dr * tc + di * ts, di * tc - dr * ts], 0))
        out = dot_stacked(g1b[...], g1h[...], jnp.concatenate(turned, 1))
        for field in range(3):
            for h in range(2):
                for z in range(2):
                    start = (h * 2 + z) * PLANE
                    sb[series_rows(c, field, h, z), :] = out[
                        start : start + PLANE, field * HALF : (field + 1) * HALF
                    ]

    def take(pair, field, h):
        parts = [
            rb[pl.ds((pair * 2 + c) * SPAN + field * 2 + h, OWNERS, stride=TILE), :] for c in range(2)
        ]
        return jnp.concatenate(parts, 0).T

    partners = (
        {"ctx": yx * 4 + mz * 2 + 1 - core},
        {"ctx": (y * 4 + x + 1 - 2 * (x % 2)) * 4 + mz * 2 + core},
        {"ctx": (y * 4 + (x + 2) % 4) * 4 + mz * 2 + core},
        {"ctx": ((y + 1 - 2 * (y % 2)) * 4 + x) * 4 + mz * 2 + core},
        {"ctx": (((y + 2) % 4) * 4 + x) * 4 + mz * 2 + core},
        z_device,
    )

    def skip_copy(i):
        return pltpu.make_async_remote_copy(
            src_ref=skip_send.at[i], dst_ref=skip_recv.at[i], send_sem=sk_send.at[i], recv_sem=sk_recv.at[i],
            device_id=partners[i], device_id_type=MESH,
        )

    def skip_step(i):
        skip_copy(i).wait_recv()
        total = skip_send[i] + skip_recv[i]
        if i + 1 < len(partners):
            skip_send[i + 1] = total
            skip_copy(i + 1).start()
        else:
            gs[...] = jnp.sum(total, axis=0, keepdims=True) * (1.0 / HALF)

    for i in range(5):
        loads[i].wait()
    lay_out(sa, 0)
    pl.semaphore_wait(barrier, 8)
    cross(0)
    cross(1)
    signal(column_sem, column)
    lay_out(sa, 1)
    cross(2)
    pl.semaphore_wait(column_sem, 3)
    signal(core_sem, [core_device])
    pl.semaphore_wait(core_sem, 1)
    signal(plane_sem, [z_device])
    for c in range(3):
        own_plane(c)
    total = jnp.zeros((TILE, 2 * HALF), F32)
    for i in range(4):
        at = slice(i * 64, (i + 1) * 64)
        prod = (k[at, :].astype(F32) * v[at, :].astype(F32)) * (q[at, :].astype(F32) * cot[at, :].astype(F32))
        total = total + jnp.sum(prod.reshape(8, TILE, 2 * HALF), axis=0)
    skip_send[0] = total
    skip_copy(0).start()
    for i in range(5, len(loads)):
        loads[i].wait()
    for table, high, low in ((f2, f2h, f2l), (g2, g2h, g2l)):
        high[...], low[...] = split(table[...])
    high, low = split(f1[...])
    f1h[...], f1b[...] = high, jnp.concatenate([high, low], 1)
    high, low = split(g1[...])
    g1h[...], g1b[...] = high, jnp.concatenate([high, low], 0)
    skip_step(0)
    hand_over(0)
    pl.semaphore_wait(plane_sem, 1)
    direct(sa, ra, 3, 3)
    for c in range(4):
        if c < 2:
            hand_over(c + 1)
        moved(c, recv_sem)
        transform(c)
        direct(sb, rb, 4 + c, c)
        skip_step(c + 1)

    def finish(pair):
        cols = slice(pair * HALF, (pair + 1) * HALF)
        bias = skip[:, cols]
        for h in range(2):
            at = slice(h * HALF, (h + 1) * HALF)
            qp, kp, vp, cp = [piece(ref, h, pair) for ref in (q, k, v, cot)]
            mixed = take(pair, 0, h) + bias * (kp * vp)
            gated[at, cols] = (qp * mixed).astype(BF16)
            gq[at, cols] = (cp * mixed).astype(BF16)
            grad = take(pair, 1, h) + bias * (qp * cp)
            gk[at, cols] = (grad * vp).astype(BF16)
            gv[at, cols] = (grad * kp).astype(BF16)
            gt[at, cols] = take(pair, 2, h) * (1.0 / HALF)

    moved(4, recv_sem)
    moved(5, recv_sem)
    finish(0)
    skip_step(5)
    for c in range(3):
        wait_rows(ea, PLANE * UNIT, over_send.at[c])
    for i in range(8):
        moved(i, send_sem)
    for i in range(len(partners)):
        skip_copy(i).wait_send()
    moved(6, recv_sem)
    moved(7, recv_sem)
    finish(1)


def hand_on(*refs):
    count = len(refs) // 2
    copies = [pltpu.make_async_copy(refs[i], refs[count + i], refs[-1].at[i]) for i in range(count)]
    for copy in copies:
        copy.start()
    for copy in copies:
        copy.wait()


def shards(query_proj, key_proj, value_proj, filter_taps, skip_bias, cotangent):
    consts = [jnp.asarray(t) for t in tables()]
    shape = query_proj.shape
    args = (query_proj, key_proj, value_proj, filter_taps, skip_bias.reshape(1, -1), cotangent, *consts)
    outs = [jax.ShapeDtypeStruct(shape, BF16)] * 4 + [
        jax.ShapeDtypeStruct(shape, F32),
        jax.ShapeDtypeStruct((1, shape[1]), F32),
    ]
    anywhere = pl.BlockSpec(memory_space=pl.ANY)
    vmem = lambda *s: pltpu.VMEM(s, F32)
    dma = pltpu.SemaphoreType.DMA
    results = pl.pallas_call(
        kernel,
        out_shape=[pltpu.VMEM(o.shape, o.dtype) for o in outs],
        in_specs=[anywhere] * len(args),
        out_specs=[pl.BlockSpec(memory_space=pltpu.VMEM)] * len(outs),
        scratch_shapes=[pltpu.VMEM(a.shape, a.dtype) for a in args]
        + [vmem(ROWS, HALF)] * 4
        + [vmem(3 * PLANE * TILE, HALF)]
        + [vmem(6, TILE, 2 * HALF)] * 2
        + [
            pltpu.VMEM(s, BF16)
            for s in ((256, 128), (256, 256), (256, 256), (256, 256), (128, 256), (256, 256), (256, 256), (256, 256))
        ]
        + [dma((12,)), dma((8,)), dma((8,)), dma((6,)), dma((6,)), dma((3,)), dma((3, 4))]
        + [pltpu.SemaphoreType.REGULAR] * 3,
        compiler_params=pltpu.CompilerParams(
            collective_id=0, has_side_effects=True, vmem_limit_bytes=56 * 1024 * 1024
        ),
        name="long_conv",
    )(*args)
    gated, grad_query, grad_key, grad_value, grad_taps, grad_skip = pl.pallas_call(
        hand_on,
        out_shape=outs,
        in_specs=[pl.BlockSpec(memory_space=pltpu.VMEM)] * len(outs),
        out_specs=[anywhere] * len(outs),
        scratch_shapes=[dma((len(outs),))],
        compiler_params=pltpu.CompilerParams(vmem_limit_bytes=56 * 1024 * 1024),
        name="hand_on",
    )(*[pltpu.with_memory_space_constraint(r, pltpu.VMEM) for r in results])
    return gated, grad_query, grad_key, grad_value, grad_taps, grad_skip.reshape(-1)


def solution(mesh):
    s = P("ctx", "tp")
    return jax.shard_map(
        shards, mesh=mesh, in_specs=(s, s, s, s, P("tp"), s), out_specs=(s, s, s, s, s, P("tp")), check_vma=False
    )
```

```python
import math

import jax
import jax.numpy as jnp
import numpy as np
from jax import lax
from jax.experimental import pallas as pl
from jax.experimental.pallas import tpu as pltpu
from jax.sharding import PartitionSpec as P

MESH = pl.DeviceIdType.MESH
F32 = jnp.float32
BF16 = jnp.bfloat16
HALF = 128
PLANE = 32
TILE = 8
OWNERS = 2 * PLANE
UNIT = 6
FAR_FIRST = (2, 1, 3, 0)
SPAN = OWNERS * TILE
ROWS = 4 * SPAN


def tables():
    half, z, source = np.meshgrid(np.arange(2), np.arange(2), np.arange(PLANE), indexing="ij")
    block = (source // 2) * 4 + z * 2 + source % 2
    n1 = (block * 2 + half).reshape(-1)
    k1 = np.arange(HALF) + 0.5
    n2 = np.arange(HALF)
    period = 2 * HALF * HALF
    first = 2 * np.pi * np.outer(k1, n1) / (2 * HALF)
    twist = 2 * np.pi * np.outer(k1, n2) / period
    second = 2 * np.pi * np.outer(n2, np.arange(HALF)) / HALF
    c2, s2 = np.cos(second), np.sin(second)
    f1 = np.concatenate([np.cos(first), -np.sin(first)], 0)
    f2 = np.block([[c2, -s2], [s2, c2]])
    g2 = np.block([[c2, s2], [-s2, c2]])
    g1 = np.concatenate([np.cos(first).T, -np.sin(first).T], 1) * (2 / period)
    return [t.astype(np.float32) for t in (f1, f2, g1, g2, np.cos(twist), -np.sin(twist))]


def split(x):
    high = x.astype(BF16)
    return high, (x - high.astype(F32)).astype(BF16)


def dot(a, b):
    return jnp.dot(a, b, preferred_element_type=F32)


def dot_left(first, second, x):
    high, low = split(x)
    return dot(first, jnp.concatenate([high, high], 0)) + dot(second, low)


def dot_right(x, high_table, low_table):
    high, low = split(x)
    count = x.shape[0]
    both = dot(jnp.concatenate([high, low], 0), high_table)
    return both[:count] + (both[count:] + dot(high, low_table))


def dot_stacked(both_tables, high_table, x):
    high, low = split(x)
    both = dot(both_tables, high)
    count = high_table.shape[0]
    return both[:count] + (both[count:] + dot(high_table, low))


def kernel(
    q_in, k_in, v_in, taps_in, skip_in, cot_in,
    f1_in, f2_in, g1_in, g2_in, tr_in, ti_in,
    gated, gq, gk, gv, gt, gs,
    q, k, v, taps, skip, cot,
    f1, f2, g1, g2, tr, ti,
    sa, sb, ra, rb, ea,
    skip_send, skip_recv, f1h, f1b, f2h, f2l, g1h, g1b, g2h, g2l,
    load_sem, send_sem, recv_sem, sk_send, sk_recv, over_send, over_recv, column_sem, core_sem, plane_sem,
):
    ctx = lax.axis_index("ctx")
    core, mz, yx = ctx % 2, (ctx // 2) % 2, ctx // 4
    oz = 1 - mz
    me = yx * 2 + core
    yblk, m8 = me // 8, me % 8
    x, y = yx % 4, yx // 4

    def device(z, p):
        return {"ctx": (p // 2) * 4 + z * 2 + p % 2}

    def peer(dy, t):
        a = 2 + 3 * (t // 2)
        dx = jnp.where(t >= 4, 3 - a % 4, a % 4)
        return ((y + dy) % 4 * 4 + (x + dx) % 4) * 2 + (core + 1 - t % 2) % 2

    def to_plane(action, z, self_too=False):
        for dy in FAR_FIRST:

            def body(t, carry, dy=dy):
                action(z, peer(dy, t))
                return carry

            lax.fori_loop(0, 8 if self_too or dy else 7, body, 0)

    def to_others(action):
        for dy in FAR_FIRST:

            def body(t, carry, dy=dy):
                p = peer(dy, t)
                action(oz, p)
                action(mz, p)
                return carry

            lax.fori_loop(0, 8 if dy else 7, body, 0)
        action(oz, me)

    z_device = {"ctx": yx * 4 + oz * 2 + core}
    core_device = {"ctx": yx * 4 + mz * 2 + 1 - core}
    row = [{"ctx": (y * 4 + (x + d) % 4) * 4 + mz * 2 + core} for d in (2, 1, 3)]
    column = [{"ctx": ((y + d) % 4 * 4 + x) * 4 + mz * 2 + core} for d in (2, 1, 3)]

    def signal(sem, devices):
        for target in devices:
            pl.semaphore_signal(sem, inc=1, device_id=target, device_id_type=MESH)

    def part(owner, c):
        return pl.ds(pl.multiple_of(c * SPAN + owner * TILE, TILE), UNIT)

    barrier = pltpu.get_barrier_semaphore()

    sources = (k_in, v_in, taps_in, q_in, cot_in, f1_in, f2_in, g2_in, g1_in, tr_in, ti_in, skip_in)
    targets = (k, v, taps, q, cot, f1, f2, g2, g1, tr, ti, skip)
    loads = [pltpu.make_async_copy(s, t, load_sem.at[i]) for i, (s, t) in enumerate(zip(sources, targets))]
    for load in loads[:5]:
        load.start()
    signal(barrier, [z_device, *column, *row, core_device])
    for load in loads[5:]:
        load.start()

    def wait_rows(ref, count, sem):
        pltpu.make_async_copy(ref.at[pl.ds(0, count)], ref.at[pl.ds(0, count)], sem).wait()

    def give(src, at, dst, i, c, z, p, source):
        pltpu.make_async_remote_copy(
            src_ref=src.at[at],
            dst_ref=dst.at[part(source * PLANE + me, c)],
            send_sem=send_sem.at[i],
            recv_sem=recv_sem.at[i],
            device_id=device(z, p),
            device_id_type=MESH,
        ).start()

    def keep(src, at, dst, c, source):
        dst[part(source * PLANE + me, c), :] = src[at, :]

    def parked(p, c):
        return pl.ds(pl.multiple_of((c * PLANE + p) * TILE, TILE), UNIT)

    def cross(c):
        for k, dy in enumerate(FAR_FIRST):

            def one(t, carry, k=k, dy=dy):
                p = peer(dy, t)
                pltpu.make_async_remote_copy(
                    src_ref=sa.at[part(oz * PLANE + p, c)],
                    dst_ref=ea.at[parked(p, c)],
                    send_sem=over_send.at[c],
                    recv_sem=over_recv.at[c, k],
                    device_id=z_device,
                    device_id_type=MESH,
                ).start()
                return carry

            lax.fori_loop(0, 8, one, 0)

    def own_plane(c):
        to_plane(lambda z, p: give(sa, part(z * PLANE + p, c), ra, c, c, z, p, mz), mz)
        keep(sa, part(mz * PLANE + me, c), ra, c, mz)

    def hand_over(c):
        for k, dy in enumerate(FAR_FIRST):
            wait_rows(ea, 8 * UNIT, over_recv.at[c, k])

            def one(t, carry, dy=dy):
                p = peer(dy, t)
                give(ea, parked(p, c), ra, c, c, mz, p, oz)
                return carry

            lax.fori_loop(0, 8 if dy else 7, one, 0)
        keep(ea, parked(me, c), ra, c, oz)

    def direct(src, dst, i, c):
        to_others(lambda z, p: give(src, part(z * PLANE + p, c), dst, i, c, z, p, mz))
        keep(src, part(mz * PLANE + me, c), dst, c, mz)

    def moved(i, sem):
        count = 2 * (PLANE - 1) if i < 3 else OWNERS - 1
        wait_rows(ra, count * UNIT, sem.at[i])

    def put(s, pair, field, values, h):
        flipped = values.T
        for c in range(2):
            s[pl.ds((pair * 2 + c) * SPAN + field * 2 + h, OWNERS, stride=TILE), :] = flipped[
                c * OWNERS : (c + 1) * OWNERS
            ]

    def piece(ref, h, pair):
        return ref[h * HALF : (h + 1) * HALF, pair * HALF : (pair + 1) * HALF].astype(F32)

    def lay_out(s, pair):
        for h in range(2):
            put(s, pair, 0, piece(k, h, pair) * piece(v, h, pair), h)
            put(s, pair, 1, piece(taps, h, pair), h)
            put(s, pair, 2, piece(q, h, pair) * piece(cot, h, pair), h)

    def series_rows(c, field, h, z):
        return pl.ds(c * SPAN + z * PLANE * TILE + field * 2 + h, PLANE, stride=TILE)

    def transform(c):
        series = []
        for field in range(3):
            parts = [ra[series_rows(c, field, h, z), :] for h in range(2) for z in range(2)]
            series.append(jnp.concatenate(parts, 0))
        a = dot_left(f1b[...], f1h[...], jnp.concatenate(series, 1))
        tc, ts = tr[...], ti[...]
        turned = []
        for field in range(3):
            cols = slice(field * HALF, (field + 1) * HALF)
            ar, ai = a[:HALF, cols], a[HALF:, cols]
            turned.append(jnp.concatenate([ar * tc - ai * ts, ar * ts + ai * tc], 1))
        b = dot_right(jnp.concatenate(turned, 0), f2h[...], f2l[...])
        (ur, ui), (hr, hi), (gr, gi) = [
            (b[f * HALF : (f + 1) * HALF, :HALF], b[f * HALF : (f + 1) * HALF, HALF:]) for f in range(3)
        ]
        prods = jnp.concatenate(
            [
                jnp.concatenate([ur * hr - ui * hi, ur * hi + ui * hr], 1),
                jnp.concatenate([hr * gr + hi * gi, hr * gi - hi * gr], 1),
                jnp.concatenate([ur * gr + ui * gi, ur * gi - ui * gr], 1),
            ],
            0,
        )
        d = dot_right(prods, g2h[...], g2l[...])
        turned = []
        for field in range(3):
            at = slice(field * HALF, (field + 1) * HALF)
            dr, di = d[at, :HALF], d[at, HALF:]
            turned.append(jnp.concatenate([dr * tc + di * ts, di * tc - dr * ts], 0))
        out = dot_stacked(g1b[...], g1h[...], jnp.concatenate(turned, 1))
        for field in range(3):
            for h in range(2):
                for z in range(2):
                    start = (h * 2 + z) * PLANE
                    sb[series_rows(c, field, h, z), :] = out[
                        start : start + PLANE, field * HALF : (field + 1) * HALF
                    ]

    def take(pair, field, h):
        parts = [
            rb[pl.ds((pair * 2 + c) * SPAN + field * 2 + h, OWNERS, stride=TILE), :] for c in range(2)
        ]
        return jnp.concatenate(parts, 0).T

    partners = (
        {"ctx": yx * 4 + mz * 2 + 1 - core},
        {"ctx": (y * 4 + x + 1 - 2 * (x % 2)) * 4 + mz * 2 + core},
        {"ctx": (y * 4 + (x + 2) % 4) * 4 + mz * 2 + core},
        {"ctx": ((y + 1 - 2 * (y % 2)) * 4 + x) * 4 + mz * 2 + core},
        {"ctx": (((y + 2) % 4) * 4 + x) * 4 + mz * 2 + core},
        z_device,
    )

    def skip_copy(i):
        return pltpu.make_async_remote_copy(
            src_ref=skip_send.at[i], dst_ref=skip_recv.at[i], send_sem=sk_send.at[i], recv_sem=sk_recv.at[i],
            device_id=partners[i], device_id_type=MESH,
        )

    def skip_step(i):
        skip_copy(i).wait_recv()
        total = skip_send[i] + skip_recv[i]
        if i + 1 < len(partners):
            skip_send[i + 1] = total
            skip_copy(i + 1).start()
        else:
            gs[...] = jnp.sum(total, axis=0, keepdims=True) * (1.0 / HALF)

    for i in range(5):
        loads[i].wait()
    lay_out(sa, 0)
    pl.semaphore_wait(barrier, 8)
    cross(0)
    cross(1)
    signal(column_sem, column)
    lay_out(sa, 1)
    cross(2)
    pl.semaphore_wait(column_sem, 3)
    signal(core_sem, [core_device])
    pl.semaphore_wait(core_sem, 1)
    signal(plane_sem, [z_device])
    for c in range(3):
        own_plane(c)
    total = jnp.zeros((TILE, 2 * HALF), F32)
    for i in range(4):
        at = slice(i * 64, (i + 1) * 64)
        prod = (k[at, :].astype(F32) * v[at, :].astype(F32)) * (q[at, :].astype(F32) * cot[at, :].astype(F32))
        total = total + jnp.sum(prod.reshape(8, TILE, 2 * HALF), axis=0)
    skip_send[0] = total
    skip_copy(0).start()
    for i in range(5, len(loads)):
        loads[i].wait()
    for table, high, low in ((f2, f2h, f2l), (g2, g2h, g2l)):
        high[...], low[...] = split(table[...])
    high, low = split(f1[...])
    f1h[...], f1b[...] = high, jnp.concatenate([high, low], 1)
    high, low = split(g1[...])
    g1h[...], g1b[...] = high, jnp.concatenate([high, low], 0)
    skip_step(0)
    hand_over(0)
    pl.semaphore_wait(plane_sem, 1)
    direct(sa, ra, 3, 3)
    for c in range(4):
        if c < 2:
            hand_over(c + 1)
        moved(c, recv_sem)
        transform(c)
        direct(sb, rb, 4 + c, c)
        skip_step(c + 1)

    def finish(pair):
        cols = slice(pair * HALF, (pair + 1) * HALF)
        bias = skip[:, cols]
        for h in range(2):
            at = slice(h * HALF, (h + 1) * HALF)
            qp, kp, vp, cp = [piece(ref, h, pair) for ref in (q, k, v, cot)]
            mixed = take(pair, 0, h) + bias * (kp * vp)
            gated[at, cols] = (qp * mixed).astype(BF16)
            gq[at, cols] = (cp * mixed).astype(BF16)
            grad = take(pair, 1, h) + bias * (qp * cp)
            gk[at, cols] = (grad * vp).astype(BF16)
            gv[at, cols] = (grad * kp).astype(BF16)
            gt[at, cols] = take(pair, 2, h) * (1.0 / HALF)

    moved(4, recv_sem)
    moved(5, recv_sem)
    finish(0)
    skip_step(5)
    for c in range(3):
        wait_rows(ea, PLANE * UNIT, over_send.at[c])
    for i in range(8):
        moved(i, send_sem)
    for i in range(len(partners)):
        skip_copy(i).wait_send()
    moved(6, recv_sem)
    moved(7, recv_sem)
    finish(1)


def hand_on(*refs):
    count = len(refs) // 2
    copies = [pltpu.make_async_copy(refs[i], refs[count + i], refs[-1].at[i]) for i in range(count)]
    for copy in copies:
        copy.start()
    for copy in copies:
        copy.wait()


def shards(query_proj, key_proj, value_proj, filter_taps, skip_bias, cotangent):
    consts = [jnp.asarray(t) for t in tables()]
    shape = query_proj.shape
    args = (query_proj, key_proj, value_proj, filter_taps, skip_bias.reshape(1, -1), cotangent, *consts)
    outs = [jax.ShapeDtypeStruct(shape, BF16)] * 4 + [
        jax.ShapeDtypeStruct(shape, F32),
        jax.ShapeDtypeStruct((1, shape[1]), F32),
    ]
    anywhere = pl.BlockSpec(memory_space=pl.ANY)
    vmem = lambda *s: pltpu.VMEM(s, F32)
    dma = pltpu.SemaphoreType.DMA
    results = pl.pallas_call(
        kernel,
        out_shape=[pltpu.VMEM(o.shape, o.dtype) for o in outs],
        in_specs=[anywhere] * len(args),
        out_specs=[pl.BlockSpec(memory_space=pltpu.VMEM)] * len(outs),
        scratch_shapes=[pltpu.VMEM(a.shape, a.dtype) for a in args]
        + [vmem(ROWS, HALF)] * 4
        + [vmem(3 * PLANE * TILE, HALF)]
        + [vmem(6, TILE, 2 * HALF)] * 2
        + [
            pltpu.VMEM(s, BF16)
            for s in ((256, 128), (256, 256), (256, 256), (256, 256), (128, 256), (256, 256), (256, 256), (256, 256))
        ]
        + [dma((12,)), dma((8,)), dma((8,)), dma((6,)), dma((6,)), dma((3,)), dma((3, 4))]
        + [pltpu.SemaphoreType.REGULAR] * 3,
        compiler_params=pltpu.CompilerParams(
            collective_id=0, has_side_effects=True, vmem_limit_bytes=56 * 1024 * 1024
        ),
        name="long_conv",
    )(*args)
    gated, grad_query, grad_key, grad_value, grad_taps, grad_skip = pl.pallas_call(
        hand_on,
        out_shape=outs,
        in_specs=[pl.BlockSpec(memory_space=pltpu.VMEM)] * len(outs),
        out_specs=[anywhere] * len(outs),
        scratch_shapes=[dma((len(outs),))],
        compiler_params=pltpu.CompilerParams(vmem_limit_bytes=56 * 1024 * 1024),
        name="hand_on",
    )(*[pltpu.with_memory_space_constraint(r, pltpu.VMEM) for r in results])
    return gated, grad_query, grad_key, grad_value, grad_taps, grad_skip.reshape(-1)


def solution(mesh):
    s = P("ctx", "tp")
    return jax.shard_map(
        shards, mesh=mesh, in_specs=(s, s, s, s, P("tp"), s), out_specs=(s, s, s, s, s, P("tp")), check_vma=False
    )
```
